256 devices in a mesh: pipe: 4 (over y_lo, core), vocab: 16 (over y_hi, z), dp: 4 (over x).
Axes of the slice: x: 4, y: 4 (y_hi: 2, y_lo: 2; y = y_hi * 2 + y_lo), z: 8, core: 2. Of those that a mesh axis runs over, the one named last changes fastest.
Arguments:
- hidden: bfloat16 [4, 256, 8192], P('pipe', 'dp', 'vocab'), may hold values from -40 to 40
- norm_gain: bfloat16 [8192], replicated, may hold values from 0.099609375 to 1.8984375
- head_weight: bfloat16 [8192, 65536], P(('pipe', 'dp'), 'vocab'), may hold values from -0.22097087 to 0.22097087
- targets: int32 [4, 256], P('pipe', 'dp'), may hold values from 0 to 65535
- exit_layer: int32 [4], replicated, may hold values from 1 to 80, as said below
- loss_num: int32 [4], replicated, may hold values from 1 to 8
- loss_den: int32 [4], replicated, may hold values from 1 to 8
Outputs:
- grad_hidden: bfloat16 [4, 256, 8192], P('pipe', 'dp', 'vocab')
- grad_head: bfloat16 [8192, 65536], P(('pipe', 'dp'), 'vocab')
- mean_loss: float32 [], replicated
The draws below stay inside these ranges and needn't reach their ends.
Inputs may be any that keep to these rules, and one draw needn't show every extreme that they name: `exit_layer`: strictly increasing; the last is 80.
All inputs are finite; a program needn't handle non-finite values.
Results may differ from the reference program's by a relative error of at most 0.0061.
Values may be sent and summed in bfloat16 or wider, within the bound.
No kernel may reach another device: no remote copies, remote signals or barrier semaphores. Data moves between devices by JAX's collectives and lax.ppermute only.
A program may use at most 128 MiB of HBM per device.

```python
import math
import jax
import jax.numpy as jnp
import numpy as np
from jax import lax

D = 8192
LAYERS = 80
EXITS = 4
TOKENS = 256
VOCAB = 65536


def anchor_rows(key):
    signs = jnp.where(jax.random.normal(jax.random.fold_in(key, 101), (8, D), jnp.float32) > 0.0, 1.0, -1.0)
    sizes = 0.9 + 0.2 * jax.random.uniform(jax.random.fold_in(key, 103), (8, D), jnp.float32)
    return signs * sizes


def draw_hidden(key, part):
    anchors = anchor_rows(key)
    key = jax.random.fold_in(key, 7)
    subkeys = jax.random.split(key, 5)
    row_scale = jnp.exp(jax.random.uniform(subkeys[0], (EXITS, TOKENS, 1), jnp.float32) * math.log(10.0))
    col_scale = jnp.exp(jax.random.uniform(subkeys[1], (D,), jnp.float32) * math.log(10.0))
    values = jax.random.normal(subkeys[2], (EXITS, TOKENS, D), jnp.float32) * row_scale * col_scale / 16.0
    positions = jnp.arange(8) * (TOKENS // 8)
    strength = 0.75 + 0.25 * jnp.arange(8, dtype=jnp.float32) / 7.0
    aligned = strength[:, None] * anchors + jnp.sqrt(1.0 - strength[:, None] ** 2) * jax.random.normal(subkeys[4], (8, D), jnp.float32)
    values = values.at[:, positions, :].set(aligned[None, :, :] * row_scale[:, positions, :])
    return jnp.clip(values, -40.0, 40.0).astype(jnp.bfloat16)


def draw_head_weight(key, part):
    anchors = anchor_rows(key)
    key = jax.random.fold_in(key, 11)
    factor = 3.0 / math.sqrt(D)
    values = factor * jax.random.normal(key, (D, VOCAB), jnp.float32)
    columns = jnp.arange(8) * (VOCAB // 8) + 1
    lift = 250.0 / D
    dropped = jnp.maximum(1, (1 + jnp.arange(8) % 4) * D // 250)
    keep = (jnp.arange(D)[:, None] >= dropped[None, :]).astype(jnp.float32)
    values = values.at[:, columns].set(lift * anchors.T)
    values = values.at[:, columns + 1].set(lift * anchors.T * keep)
    bound = 20.0 / math.sqrt(D)
    return jnp.clip(values, -bound, bound).astype(jnp.bfloat16)


def draw_exit_layer(key, part):
    key = jax.random.fold_in(key, 5)
    span_layers = LAYERS // EXITS
    base_layer = jnp.arange(EXITS, dtype=jnp.int32) * span_layers
    offset_draw = jax.random.randint(key, (EXITS,), 1, span_layers + 1, jnp.int32)
    layers = base_layer + offset_draw
    return jnp.where(jnp.arange(EXITS) == EXITS - 1, LAYERS, layers).astype(jnp.int32)


def touch_ends(entries, key, smallest, largest):
    dims = entries.shape
    index_at = [jax.random.randint(jax.random.fold_in(key, axis), (), 0, dims[axis]) for axis in range(len(dims))]
    entries = entries.at[tuple(index_at)].set(smallest)
    longest = dims.index(max(dims))
    index_at[longest] = (index_at[longest] + 1) % dims[longest]
    return entries.at[tuple(index_at)].set(largest)


def rank_bounds(number_of, lean):
    portions = [(1 << 20) // math.isqrt(rank ** lean) + 1 for rank in range(1, number_of + 1)]
    width = 1 + sum(portions) // (1 << 30)
    return np.cumsum(np.array([max(1, weight // width) for weight in portions]))


def ranked_ids(stream_key, extent, number_of, lean):
    listing = rank_bounds(number_of, lean)
    lot = jax.random.randint(jax.random.fold_in(stream_key, 1), extent, 0, int(listing[number_of - 1]))
    grade = jnp.searchsorted(jnp.asarray(listing, jnp.int32), lot, side="right")
    return jax.random.permutation(jax.random.fold_in(stream_key, 2), number_of)[grade].astype(jnp.int32)


def setup_inputs(seed: int = 0) -> dict:
    seeds = jax.random.split(jax.random.key(seed), 8)
    hidden = draw_hidden(jax.random.fold_in(seeds[7], 71), 0)
    norm_gain = jnp.clip(1.0 + 0.18 * jax.random.normal(seeds[1], (D,), jnp.float32), 0.099609375, 1.8984375).astype(jnp.bfloat16)
    head_weight = draw_head_weight(jax.random.fold_in(seeds[7], 71), 0)
    targets = touch_ends(ranked_ids(seeds[3], (EXITS, TOKENS), VOCAB, 2), jax.random.fold_in(seeds[3], 3), 0, VOCAB - 1).astype(jnp.int32)
    exit_layer = draw_exit_layer(jax.random.fold_in(seeds[7], 71), 0)
    loss_num = touch_ends(jax.random.randint(seeds[5], (EXITS,), 1, 9), jax.random.fold_in(seeds[5], 1), 1, 8).astype(jnp.int32)
    loss_den = touch_ends(jax.random.randint(seeds[6], (EXITS,), 1, 9), jax.random.fold_in(seeds[6], 1), 1, 8).astype(jnp.int32)
    return dict(hidden=hidden, norm_gain=norm_gain, head_weight=head_weight, targets=targets, exit_layer=exit_layer, loss_num=loss_num, loss_den=loss_den)


def reference(hidden, norm_gain, head_weight, targets, exit_layer, loss_num, loss_den):
    row_count = EXITS * TOKENS
    widened = hidden.reshape(row_count, D).astype(jnp.float32)
    gain_f32 = norm_gain.astype(jnp.float32)
    inv_rms = lax.rsqrt(lax.optimization_barrier(jnp.mean(widened * widened, axis=1)) + 1e-05)
    normed = (widened * inv_rms[:, None] * gain_f32).astype(jnp.bfloat16)
    logits = jnp.dot(normed, head_weight, preferred_element_type=jnp.float32)
    peak_value = lax.optimization_barrier(jnp.max(logits, axis=1))
    total_sum = lax.optimization_barrier(jnp.sum(jnp.exp(logits - peak_value[:, None]), axis=1))
    log_total = peak_value + jnp.log(total_sum)
    target_hit = lax.broadcasted_iota(jnp.int32, (1, VOCAB), 1) == targets.reshape(row_count, 1).astype(jnp.int32)
    chosen = lax.optimization_barrier(jnp.sum(jnp.where(target_hit, logits, jnp.zeros_like(logits)), axis=1))
    ratio_value = loss_num.astype(jnp.float32) / loss_den.astype(jnp.float32)
    scale_value = ratio_value * jnp.exp2(exit_layer.astype(jnp.float32) / LAYERS)
    weight = scale_value * (EXITS / jnp.sum(scale_value))
    row_weight = jnp.repeat(weight, TOKENS)
    mean_loss = jnp.sum(row_weight * (log_total - chosen)) / TOKENS
    probability = jnp.exp(logits - log_total[:, None])
    grad_logits = (row_weight[:, None] * (probability - target_hit.astype(jnp.float32))).astype(jnp.bfloat16)
    grad_head = lax.dot_general(normed, grad_logits, (((0,), (0,)), ((), ())), preferred_element_type=jnp.float32).astype(jnp.bfloat16)
    grad_normed = lax.dot_general(grad_logits, head_weight, (((1,), (1,)), ((), ())), preferred_element_type=jnp.float32)
    inner_total = lax.optimization_barrier(jnp.sum(grad_normed * gain_f32 * widened, axis=1))
    grad_hidden = inv_rms[:, None] * gain_f32 * grad_normed - widened * (inv_rms ** 3 * inner_total / D)[:, None]
    return (grad_hidden.astype(jnp.bfloat16).reshape(EXITS, TOKENS, D), grad_head, mean_loss)
```

```python
import jax
import jax.numpy as jnp
from jax import lax
from jax.sharding import Mesh, PartitionSpec as P

LAYERS = 80
EPS = 1e-05
F32 = jnp.float32
BF16 = jnp.bfloat16
AXES = ("yl", "core", "yh", "z", "x")
SWAP = [(0, 1), (1, 0)]


def place(group, vocab):
    return ((group // 4) * 16 + vocab) * 4 + group % 4


TRANSPOSE = [(place(g, v), place(v, g)) for g in range(16) for v in range(16)]


def transpose_groups(block):
    return lax.ppermute(block, AXES, TRANSPOSE)


def shift_x(block, step):
    return lax.ppermute(block, "x", [(i, (i + step) % 4) for i in range(4)])


def swap_y(block):
    return lax.ppermute(block, "yl", SWAP)


def swap_core(block):
    return lax.ppermute(block, "core", SWAP)


def exit_weights(exit_layer, loss_num, loss_den):
    ratio_value = loss_num.astype(F32) / loss_den.astype(F32)
    scale_value = ratio_value * jnp.exp2(exit_layer.astype(F32) / LAYERS)
    return scale_value * (scale_value.shape[0] / jnp.sum(scale_value))


def ring_sum(own, right, left, far):
    half = far.shape[-1] // 2
    from_left = shift_x(far[..., :half], 1)
    from_right = shift_x(far[..., half:], -1)
    right = jnp.concatenate([right[..., :half] + from_left, right[..., half:]], -1)
    left = jnp.concatenate([left[..., :half], left[..., half:] + from_right], -1)
    return own + shift_x(right, 1) + shift_x(left, -1)


def gather_group(block):
    half = block.shape[0] // 2
    left = shift_x(block, 1)
    right = shift_x(block, -1)
    over = swap_y(block)
    far = jnp.concatenate([shift_x(left[:half], 1), shift_x(right[half:], -1)])
    over_right = swap_y(right)
    over_left = shift_x(over, 1)
    over_far = jnp.concatenate([swap_y(far[:half]), shift_x(over_right[half:], -1)])
    return ((0, 0, block), (0, -1, left), (0, 1, right), (0, 2, far)), (
        (1, 0, over),
        (1, -1, over_left),
        (1, 1, over_right),
        (1, 2, over_far),
    )


def butterfly_sum(values):
    values = values + swap_y(values)
    for bit in (1, 2):
        values = values + lax.ppermute(values, "x", [(i, i ^ bit) for i in range(4)])
    return values


def butterfly_gather(values):
    for axis, bit, size in (("x", 1, 4), ("x", 2, 4), ("core", 1, 2), ("yl", 1, 2)):
        other = lax.ppermute(values, axis, [(i, i ^ bit) for i in range(size)])
        high = (lax.axis_index(axis) & bit) > 0
        values = jnp.concatenate(
            [jnp.where(high, other, values), jnp.where(high, values, other)], 0
        )
    return values


def shards(hidden, norm_gain, head_weight, targets, exit_layer, loss_num, loss_den):
    yl, core, yh, z, x = (lax.axis_index(name) for name in AXES)
    vocab = yh * 8 + z
    group = (yl * 2 + core) * 4 + x
    own = hidden[0]
    tok, wide = own.shape
    rows = 16 * tok
    part = 2 * tok
    cols = head_weight.shape[1] // 2
    width = 16 * wide
    gain = norm_gain.astype(F32)

    kept = lax.dynamic_slice_in_dim(head_weight, core * cols, cols, 1)
    given = lax.dynamic_slice_in_dim(head_weight, (1 - core) * cols, cols, 1)
    head = jnp.concatenate([kept, swap_core(given)], 0)

    moved = transpose_groups(own)
    feature_rows = lax.all_to_all(
        jnp.broadcast_to(moved[None], (16, tok, wide)), ("yh", "z"), 0, 0, tiled=True
    ).reshape(rows, wide)
    partner_rows = swap_core(feature_rows)
    pair_rows = jnp.concatenate([feature_rows, partner_rows], 1)
    partner_group = (yl * 2 + 1 - core) * 4 + x
    pair_gain = jnp.concatenate(
        [
            lax.dynamic_slice_in_dim(gain, group * wide, wide),
            lax.dynamic_slice_in_dim(gain, partner_group * wide, wide),
        ]
    )
    pair_f32 = pair_rows.astype(F32)
    scaled = (pair_f32 * pair_gain).astype(BF16)

    def rows_of(source, dy, dx):
        index = (yl ^ dy) * 4 + ((x + dx) & 3)
        return lax.dynamic_slice_in_dim(source, index * part, part, 0)

    squares = butterfly_sum(jnp.sum(pair_f32 * pair_f32, axis=1).reshape(8, part))
    inv_rms = lax.rsqrt(squares / width + EPS)

    near = jnp.concatenate([rows_of(scaled, 0, dx) for dx in (0, 1, -1, 2)], 0)
    over = jnp.concatenate([rows_of(scaled, 1, dx) for dx in (0, 1, -1, 2)], 0)
    half = cols // 2

    def product(source, columns):
        return jnp.dot(source, columns, preferred_element_type=F32).reshape(4, part, half)

    over_a = product(over, head[:, :half])
    over_b = product(over, head[:, half:])
    near_b = product(near, head[:, half:])
    near_a = product(near, head[:, :half])
    sum_a = near_a + swap_y(over_a)
    far_b = ring_sum(over_b[0], over_b[1], over_b[2], over_b[3])
    sum_b = ring_sum(near_b[0], near_b[1], near_b[2], near_b[3]) + swap_y(far_b)
    sum_a = ring_sum(sum_a[0], sum_a[1], sum_a[2], sum_a[3])

    block = yl * 4 + x
    all_targets = butterfly_gather(targets).reshape(8, part)
    own_targets = lax.dynamic_index_in_dim(all_targets, block, 0, False)
    own_inv = lax.dynamic_index_in_dim(inv_rms, block, 0, False)
    logits = jnp.concatenate([sum_a, sum_b], 1) * own_inv[:, None]
    columns = vocab * (2 * cols) + core * cols + lax.broadcasted_iota(jnp.int32, (1, cols), 1)
    hit = columns == own_targets[:, None]
    peak = jnp.max(logits, axis=1)
    lowered = logits - peak[:, None]
    power = jnp.exp(lowered)
    total = jnp.sum(power, axis=1)
    moment = jnp.sum(power * lowered, axis=1)
    chosen = jnp.sum(jnp.where(hit, logits, 0.0), axis=1)
    marked = jnp.where(hit, -1.0, power).astype(BF16)

    stats = jnp.stack([peak, total, moment, chosen])
    spread = lax.all_to_all(
        jnp.broadcast_to(stats[None], (256, 4, part)), AXES, 0, 0, tiled=True
    ).reshape(2, 2, 16, 4, 4, part)
    near_blocks, over_blocks = gather_group(marked)

    def by_block(values):
        return values.transpose(0, 3, 1, 2, 4).reshape(8, 32, part)

    peaks = by_block(spread[:, :, :, :, 0])
    totals = by_block(spread[:, :, :, :, 1])
    moments = by_block(spread[:, :, :, :, 2])
    chosen_all = jnp.sum(by_block(spread[:, :, :, :, 3]), axis=1)
    top = jnp.max(peaks, axis=1)
    below = peaks - top[:, None]
    factor = jnp.exp(below)
    total_sum = jnp.sum(totals * factor, axis=1)
    moment_sum = jnp.sum(factor * (moments + totals * below), axis=1)
    log_sum = jnp.log(total_sum)
    log_total = top + log_sum
    weight = exit_weights(exit_layer, loss_num, loss_den)
    row_weight = jnp.repeat(weight, 2)[:, None]
    mean_loss = jnp.sum(row_weight * (log_total - chosen_all)) / (4 * tok)
    slope = row_weight * (moment_sum / total_sum + (top - chosen_all))
    own_peaks = lax.dynamic_index_in_dim(peaks, core * 16 + vocab, 1, False)
    ratio = row_weight * jnp.exp(own_peaks - log_total)
    at_target = row_weight * (jnp.exp(chosen_all - log_total) - 1.0)

    grad_logits = jnp.zeros((rows, cols), BF16)
    for dy, dx, piece in near_blocks + over_blocks:
        index = (yl ^ dy) * 4 + ((x + dx) & 3)
        scale = lax.dynamic_index_in_dim(ratio, index, 0, False)[:, None]
        special = lax.dynamic_index_in_dim(at_target, index, 0, False)[:, None]
        value = piece.astype(F32)
        value = jnp.where(value < 0.0, special, value * scale).astype(BF16)
        grad_logits = lax.dynamic_update_slice_in_dim(grad_logits, value, index * part, 0)

    def feature_gradient(source):
        return lax.dot_general(
            grad_logits, source, (((1,), (1,)), ((), ())), preferred_element_type=F32
        )

    for_partner = feature_gradient(head[wide:])
    for_own = feature_gradient(head[:wide])
    chip_sum = for_own + swap_core(for_partner)
    returned = lax.all_to_all(
        chip_sum.astype(BF16).reshape(16, tok, wide), ("yh", "z"), 0, 0, tiled=True
    )
    feature_grad = transpose_groups(jnp.sum(returned.astype(F32), axis=0))

    normed = (pair_f32 * inv_rms.reshape(rows)[:, None] * pair_gain).astype(BF16)
    head_grad = lax.dot_general(
        normed, grad_logits, (((0,), (0,)), ((), ())), preferred_element_type=F32
    ).astype(BF16)
    head_own = head_grad[:wide]
    head_other = swap_core(head_grad[wide:])
    first = core == 0
    grad_head = jnp.concatenate(
        [jnp.where(first, head_own, head_other), jnp.where(first, head_other, head_own)], 1
    )

    def of_group(values):
        return lax.dynamic_slice_in_dim(values.reshape(rows), group * tok, tok)[:, None]

    row_inv = of_group(inv_rms)
    gain_slice = lax.dynamic_slice_in_dim(gain, vocab * wide, wide)
    grad_hidden = row_inv * gain_slice * feature_grad - own.astype(F32) * (
        row_inv * row_inv * of_group(slope) / width
    )
    return grad_hidden.astype(BF16)[None], grad_head, mean_loss


def solution(mesh):
    fine = Mesh(mesh.devices.reshape(2, 2, 2, 8, 4), AXES)
    slab, entry = ("yl", "core"), ("yh", "z")
    in_specs = (
        P(slab, "x", entry),
        P(),
        P(slab + ("x",), entry),
        P(slab, "x"),
        P(),
        P(),
        P(),
    )
    out_specs = (P(slab, "x", entry), P(slab + ("x",), entry), P())
    return jax.shard_map(shards, mesh=fine, in_specs=in_specs, out_specs=out_specs, check_vma=False)
```

```python
import jax
import jax.numpy as jnp
from jax import lax
from jax.experimental import pallas as pl
from jax.experimental.pallas import tpu as pltpu
from jax.sharding import Mesh, PartitionSpec as P

LAYERS = 80
EPS = 1e-05
F32 = jnp.float32
BF16 = jnp.bfloat16
AXES = ("yl", "core", "yh", "z", "x")
SWAP = [(0, 1), (1, 0)]


def place(group, vocab):
    return ((group // 4) * 16 + vocab) * 4 + group % 4


TRANSPOSE = [(place(g, v), place(v, g)) for g in range(16) for v in range(16)]


def transpose_groups(block):
    return lax.ppermute(block, AXES, TRANSPOSE)


def shift_x(block, step):
    return lax.ppermute(block, "x", [(i, (i + step) % 4) for i in range(4)])


def swap_y(block):
    return lax.ppermute(block, "yl", SWAP)


def swap_core(block):
    return lax.ppermute(block, "core", SWAP)


def flip(block, axis, bit, size):
    return lax.ppermute(block, axis, [(i, i ^ bit) for i in range(size)])


def in_pair(mine, other, axis, bit):
    high = (lax.axis_index(axis) & bit) > 0
    return jnp.where(high, other, mine), jnp.where(high, mine, other)


def exit_weights(exit_layer, loss_num, loss_den):
    ratio_value = loss_num.astype(F32) / loss_den.astype(F32)
    scale_value = ratio_value * jnp.exp2(exit_layer.astype(F32) / LAYERS)
    return scale_value * (scale_value.shape[0] / jnp.sum(scale_value))


def gather_group(block):
    half = block.shape[0] // 2
    left = shift_x(block, 1)
    right = shift_x(block, -1)
    over = swap_y(block)
    far = jnp.concatenate([shift_x(left[:half], 1), shift_x(right[half:], -1)])
    over_right = swap_y(right)
    over_left = shift_x(over, 1)
    over_far = jnp.concatenate([swap_y(far[:half]), shift_x(over_right[half:], -1)])
    return {
        (0, 0): block,
        (0, -1): left,
        (0, 1): right,
        (0, 2): far,
        (1, 0): over,
        (1, -1): over_left,
        (1, 1): over_right,
        (1, 2): over_far,
    }


def gather_rows(values):
    for axis, bit, size in (("x", 1, 4), ("x", 2, 4), ("yl", 1, 2)):
        values = jnp.concatenate(in_pair(values, flip(values, axis, bit, size), axis, bit), 0)
    return values


def combine_stats(stats):
    for axis, bit, size in (("core", 1, 2), ("z", 1, 8), ("z", 2, 8), ("z", 4, 8), ("yh", 1, 2)):
        low, high = in_pair(stats, flip(stats, axis, bit, size), axis, bit)
        top = jnp.maximum(low[0], high[0])
        low_gap, high_gap = low[0] - top, high[0] - top
        low_factor, high_factor = jnp.exp(low_gap), jnp.exp(high_gap)
        total = low[1] * low_factor + high[1] * high_factor
        moment = (low[2] + low[1] * low_gap) * low_factor
        moment = moment + (high[2] + high[1] * high_gap) * high_factor
        stats = jnp.stack([top, total, moment, low[3] + high[3]])
    return stats


EXTRA = 128
TILE = 256
SIDES = (0, 1)
SENT = ((0, 2), (1, 1), (1, 2), (0, -1))
HELD = ((0, 1), (1, -1), (0, 0), (1, 0))
Y_ORDER = ((2, 0), (1, 1), (2, 1), (-1, 0), (1, 0), (-1, 1), (0, 0), (0, 1))


def x_spots(pairs):
    return [(dy, dx, side) for dy, dx in pairs for side in SIDES]


def y_spots(dy):
    return [(dy, dx, side) for dx, side in Y_ORDER]


def logits_kernel(
    spot_ref, own_ref, partner_ref, gain_ref, head_ref, x_ref, y_ref, x_rows, y_rows
):
    tok, wide = own_ref.shape[1:]
    cut = y_ref.shape[1] - EXTRA
    for index in range(8):
        x_spot, y_spot = spot_ref[index], spot_ref[8 + index]
        rows = pl.ds(index * tok, tok)
        squares = jnp.zeros((tok, 1), F32)
        for source, half in ((own_ref, 0), (partner_ref, 1)):
            lanes = pl.ds(half * wide, wide)
            gain = gain_ref[:, lanes]
            x_rows[rows, lanes] = (source[x_spot].astype(F32) * gain).astype(BF16)
            block = source[y_spot].astype(F32)
            y_rows[rows, lanes] = (block * gain).astype(BF16)
            squares = squares + jnp.sum(block * block, axis=1, keepdims=True)
        y_ref[rows, cut:] = jnp.broadcast_to(squares, (tok, EXTRA))

    def step_into(out_ref, lhs_ref, start):
        def step(index, carry):
            lanes = pl.ds(pl.multiple_of(index * TILE, TILE), TILE)
            columns = head_ref[:, pl.ds(pl.multiple_of(start + index * TILE, TILE), TILE)]
            out_ref[:, lanes] = jnp.dot(lhs_ref[...], columns, preferred_element_type=F32)
            return carry

        return step

    lax.fori_loop(0, cut // TILE, step_into(y_ref, y_rows, 0), 0)
    lax.fori_loop(0, x_ref.shape[1] // TILE, step_into(x_ref, x_rows, cut), 0)


def partial_logits(spots, own_rows, partner_rows, pair_gain, head, cut):
    rows = own_rows.shape[0] * own_rows.shape[1] // 2
    depth, cols = head.shape
    whole = pl.BlockSpec(memory_space=pltpu.VMEM)
    return pl.pallas_call(
        logits_kernel,
        out_shape=(
            jax.ShapeDtypeStruct((rows, cols - cut), F32),
            jax.ShapeDtypeStruct((rows, cut + EXTRA), F32),
        ),
        in_specs=[pl.BlockSpec(memory_space=pltpu.SMEM)] + [whole] * 4,
        out_specs=(whole, whole),
        scratch_shapes=[pltpu.VMEM((rows, depth), BF16), pltpu.VMEM((rows, depth), BF16)],
        compiler_params=pltpu.CompilerParams(vmem_limit_bytes=40 * 2**20),
        cost_estimate=pl.CostEstimate(
            flops=2 * rows * depth * cols, bytes_accessed=12 * 2**20, transcendentals=0
        ),
    )(spots, own_rows, partner_rows, pair_gain[None], head)


def shards(hidden, norm_gain, head_weight, targets, exit_layer, loss_num, loss_den):
    yl, core, yh, z, x = (lax.axis_index(name) for name in AXES)
    vocab = yh * 8 + z
    group = (yl * 2 + core) * 4 + x
    own = hidden[0]
    tok, wide = own.shape
    cols = head_weight.shape[1] // 2
    width = 16 * wide
    gain = norm_gain.astype(F32)
    weight = exit_weights(exit_layer, loss_num, loss_den)

    own_f32 = own.astype(F32)
    pair_targets = jnp.stack(in_pair(targets[0], swap_core(targets[0]), "core", 1))
    moved, head_weight = lax.optimization_barrier((transpose_groups(own), head_weight))
    kept = lax.dynamic_slice_in_dim(head_weight, core * cols, cols, 1)
    given = lax.dynamic_slice_in_dim(head_weight, (1 - core) * cols, cols, 1)
    received = swap_core(given)
    feature_rows = lax.all_to_all(
        jnp.broadcast_to(moved[None], (16, tok, wide)), ("yh", "z"), 0, 0, tiled=True
    )
    head = jnp.concatenate([kept, received], 0)
    feature_rows, pair_targets, head = lax.optimization_barrier(
        (feature_rows, pair_targets, head)
    )
    partner_rows = swap_core(feature_rows)
    partner_group = (yl * 2 + 1 - core) * 4 + x
    pair_gain = jnp.concatenate(
        [
            lax.dynamic_slice_in_dim(gain, group * wide, wide),
            lax.dynamic_slice_in_dim(gain, partner_group * wide, wide),
        ]
    )
    part = 2 * tok
    cut = (cols * 3 // 8) // TILE * TILE

    def partials(pairs, dy):
        spots = jnp.stack(
            [
                ((yl ^ to_y) * 2 + side) * 4 + ((x + to_x) & 3)
                for to_y, to_x, side in x_spots(pairs) + y_spots(dy)
            ]
        ).astype(jnp.int32)
        return partial_logits(spots, feature_rows, partner_rows, pair_gain, head, cut)

    leaving, over = partials(SENT, 1)
    staying, near = partials(HELD, 0)

    from_left, from_right = lax.optimization_barrier(
        (shift_x(leaving[: 2 * part], 1), shift_x(leaving[2 * part :], -1))
    )
    right0, left1 = lax.optimization_barrier(
        (staying[:part] + from_left[:part], staying[part : 2 * part] + from_right[:part])
    )
    own0 = staying[2 * part : 3 * part] + from_right[part:]
    own1 = staying[3 * part :] + from_left[part:]
    own0 = own0 + shift_x(right0, 1)
    own1 = own1 + shift_x(left1, -1)
    near = near + swap_y(over)
    own0, own1, near = lax.optimization_barrier((own0, own1, near))

    from_left, from_right, from_over = lax.optimization_barrier(
        (shift_x(near[:part], 1), shift_x(near[part : 2 * part], -1), swap_y(own1[:tok]))
    )
    right = near[2 * part : 2 * part + tok] + from_left[:tok]
    left = near[2 * part + tok : 3 * part] + from_right[:tok]
    upper = near[3 * part : 3 * part + tok] + from_right[tok:]
    lower = near[3 * part + tok :] + from_left[tok:]
    right, left = lax.optimization_barrier((right, left))
    y_sum = jnp.concatenate([upper + shift_x(right, 1), lower + shift_x(left, -1)], 0)
    x_sum = own0 + jnp.concatenate([from_over, swap_y(own1[tok:])], 0)

    columns = vocab * (2 * cols) + core * cols + lax.broadcasted_iota(jnp.int32, (1, cols), 1)
    slab_weight = lax.dynamic_slice_in_dim(weight, yl * 2, 2)
    part_weight = jnp.broadcast_to(slab_weight[:, None], (2, tok)).reshape(part)

    pair_inv = lax.rsqrt(y_sum[:, cut] / width + EPS).reshape(2, tok)
    raw = jnp.concatenate([y_sum[:, :cut], x_sum], 1)
    raw, late_inv = lax.optimization_barrier((raw, pair_inv))
    all_inv = gather_rows(late_inv[None])
    logits = raw * pair_inv.reshape(part)[:, None]
    hit = columns == pair_targets.reshape(part)[:, None]
    peak = jnp.max(logits, axis=1)
    lowered = logits - peak[:, None]
    power = jnp.exp(lowered)
    total = jnp.sum(power, axis=1)
    moment = jnp.sum(power * lowered, axis=1)
    chosen = jnp.sum(jnp.where(hit, logits, 0.0), axis=1)
    top, total, moment, chosen = combine_stats(jnp.stack([peak, total, moment, chosen]))
    log_total = top + jnp.log(total)
    probability = jnp.exp(logits - log_total[:, None])
    grad_logits = (part_weight[:, None] * (probability - hit.astype(F32))).astype(BF16)
    loss = part_weight * (log_total - chosen)
    slope = (part_weight * (moment / total + (top - chosen))).reshape(2, tok)
    grad_logits, all_inv = lax.optimization_barrier((grad_logits, all_inv))

    grads = jnp.zeros((2, 2, 4, tok, cols), BF16)
    for (dy, dx), piece in gather_group(grad_logits).items():
        grads = lax.dynamic_update_slice(
            grads, piece.reshape(1, 2, 1, tok, cols), (yl ^ dy, 0, (x + dx) & 3, 0, 0)
        )
    grads = grads.reshape(16 * tok, cols)

    def partial(source):
        return lax.dot_general(
            grads, source, (((1,), (1,)), ((), ())), preferred_element_type=F32
        )

    for_partner = partial(head[wide:]).astype(BF16)
    for_own = lax.optimization_barrier(partial(head[:wide]))
    chip_sum = (for_own + swap_core(for_partner).astype(F32)).astype(BF16)
    chip_sum, all_inv = lax.optimization_barrier((chip_sum, all_inv))
    returned = lax.all_to_all(chip_sum.reshape(16, tok, wide), ("yh", "z"), 0, 0, tiled=True)
    feature_grad = transpose_groups(jnp.sum(returned.astype(F32), axis=0))
    inv_rms = all_inv.reshape(2, 4, 2, tok).transpose(0, 2, 1, 3).reshape(16, tok)
    pair_f32 = jnp.concatenate([feature_rows, partner_rows], 2).astype(F32)
    normed = (pair_f32 * inv_rms[:, :, None] * pair_gain).astype(BF16)
    head_grad = lax.dot_general(
        normed.reshape(16 * tok, 2 * wide),
        grads,
        (((0,), (0,)), ((), ())),
        preferred_element_type=F32,
    ).astype(BF16)
    head_grad, loss = lax.optimization_barrier((head_grad, loss))
    mean_loss = jnp.sum(gather_rows(loss.reshape(1, part))) / (4 * tok)
    head_own = head_grad[:wide]
    head_other = swap_core(head_grad[wide:])
    grad_head = jnp.concatenate(in_pair(head_own, head_other, "core", 1), 1)

    row_slope = lax.dynamic_index_in_dim(slope, core, 0, False)
    row_inv = lax.dynamic_index_in_dim(pair_inv, core, 0, False)
    gain_slice = lax.dynamic_slice_in_dim(gain, vocab * wide, wide)
    grad_hidden = row_inv[:, None] * gain_slice * feature_grad - own_f32 * (
        row_inv * row_inv * row_slope / width
    )[:, None]
    return grad_hidden.astype(BF16)[None], grad_head, mean_loss


def solution(mesh):
    fine = Mesh(mesh.devices.reshape(2, 2, 2, 8, 4), AXES)
    slab, entry = ("yl", "core"), ("yh", "z")
    in_specs = (
        P(slab, "x", entry),
        P(),
        P(slab + ("x",), entry),
        P(slab, "x"),
        P(),
        P(),
        P(),
    )
    out_specs = (P(slab, "x", entry), P(slab + ("x",), entry), P())
    return jax.shard_map(shards, mesh=fine, in_specs=in_specs, out_specs=out_specs, check_vma=False)
```

```python
import jax
import jax.numpy as jnp
from jax import lax
from jax.experimental import pallas as pl
from jax.experimental.pallas import tpu as pltpu
from jax.sharding import Mesh, PartitionSpec as P

LAYERS = 80
EPS = 1e-05
F32 = jnp.float32
BF16 = jnp.bfloat16
AXES = ("yl", "core", "yh", "z", "x")
SWAP = [(0, 1), (1, 0)]


def place(group, vocab):
    return ((group // 4) * 16 + vocab) * 4 + group % 4


TRANSPOSE = [(place(g, v), place(v, g)) for g in range(16) for v in range(16)]


def transpose_groups(block):
    return lax.ppermute(block, AXES, TRANSPOSE)


def shift_x(block, step):
    return lax.ppermute(block, "x", [(i, (i + step) % 4) for i in range(4)])


def swap_y(block):
    return lax.ppermute(block, "yl", SWAP)


def swap_core(block):
    return lax.ppermute(block, "core", SWAP)


def flip(block, axis, bit, size):
    return lax.ppermute(block, axis, [(i, i ^ bit) for i in range(size)])


def in_pair(mine, other, axis, bit):
    high = (lax.axis_index(axis) & bit) > 0
    return jnp.where(high, other, mine), jnp.where(high, mine, other)


def exit_weights(exit_layer, loss_num, loss_den):
    ratio_value = loss_num.astype(F32) / loss_den.astype(F32)
    scale_value = ratio_value * jnp.exp2(exit_layer.astype(F32) / LAYERS)
    return scale_value * (scale_value.shape[0] / jnp.sum(scale_value))


def gather_group(block):
    half = block.shape[0] // 2
    left = shift_x(block, 1)
    right = shift_x(block, -1)
    over = swap_y(block)
    far = jnp.concatenate([shift_x(left[:half], 1), shift_x(right[half:], -1)])
    over_right = swap_y(right)
    over_left = shift_x(over, 1)
    over_far = jnp.concatenate([swap_y(far[:half]), shift_x(over_right[half:], -1)])
    return {
        (0, 0): block,
        (0, -1): left,
        (0, 1): right,
        (0, 2): far,
        (1, 0): over,
        (1, -1): over_left,
        (1, 1): over_right,
        (1, 2): over_far,
    }


def gather_rows(values):
    for axis, bit, size in (("x", 1, 4), ("x", 2, 4), ("yl", 1, 2)):
        values = jnp.concatenate(in_pair(values, flip(values, axis, bit, size), axis, bit), 0)
    return values


def combine_stats(stats):
    for axis, bit, size in (("core", 1, 2), ("z", 1, 8), ("z", 2, 8), ("z", 4, 8), ("yh", 1, 2)):
        low, high = in_pair(stats, flip(stats, axis, bit, size), axis, bit)
        top = jnp.maximum(low[0], high[0])
        low_gap, high_gap = low[0] - top, high[0] - top
        low_factor, high_factor = jnp.exp(low_gap), jnp.exp(high_gap)
        total = low[1] * low_factor + high[1] * high_factor
        moment = (low[2] + low[1] * low_gap) * low_factor
        moment = moment + (high[2] + high[1] * high_gap) * high_factor
        stats = jnp.stack([top, total, moment, low[3] + high[3]])
    return stats


EXTRA = 128
TILE = 256
SIDES = (0, 1)
SENT = ((0, 2), (1, 1), (1, 2), (0, -1))
HELD = ((0, 1), (1, -1), (0, 0), (1, 0))
Y_ORDER = ((2, 0), (1, 1), (2, 1), (-1, 0), (1, 0), (-1, 1), (0, 0), (0, 1))


def x_spots(pairs):
    return [(dy, dx, side) for dy, dx in pairs for side in SIDES]


def y_spots(dy):
    return [(dy, dx, side) for dx, side in Y_ORDER]


def logits_kernel(
    spot_ref, own_ref, partner_ref, gain_ref, kept_ref, received_ref, *refs
):
    *x_refs, y_ref, x_rows, y_rows = refs
    tok, wide = own_ref.shape[1:]
    cut = y_ref.shape[1] - EXTRA
    for index in range(8):
        x_spot, y_spot = spot_ref[index], spot_ref[8 + index]
        rows = pl.ds(index * tok, tok)
        squares = jnp.zeros((tok, 1), F32)
        for source, half in ((own_ref, 0), (partner_ref, 1)):
            lanes = pl.ds(half * wide, wide)
            gain = gain_ref[:, lanes]
            x_rows[rows, lanes] = (source[x_spot].astype(F32) * gain).astype(BF16)
            block = source[y_spot].astype(F32)
            y_rows[rows, lanes] = (block * gain).astype(BF16)
            squares = squares + jnp.sum(block * block, axis=1, keepdims=True)
        y_ref[rows, cut:] = jnp.broadcast_to(squares, (tok, EXTRA))

    def product(lhs_ref, rows, columns):
        first = jnp.dot(lhs_ref[rows, :wide], kept_ref[:, columns], preferred_element_type=F32)
        return first + jnp.dot(
            lhs_ref[rows, wide:], received_ref[:, columns], preferred_element_type=F32
        )

    def y_step(index, carry):
        lanes = pl.ds(pl.multiple_of(index * TILE, TILE), TILE)
        y_ref[:, lanes] = product(y_rows, slice(None), lanes)
        return carry

    def x_step(index, carry):
        lanes = pl.ds(pl.multiple_of(index * TILE, TILE), TILE)
        columns = pl.ds(pl.multiple_of(cut + index * TILE, TILE), TILE)
        out = product(x_rows, slice(None), columns)
        size = x_refs[0].shape[0]
        for place, x_ref in enumerate(x_refs):
            x_ref[:, lanes] = out[place * size : (place + 1) * size]
        return carry

    lax.fori_loop(0, cut // TILE, y_step, 0, unroll=True)
    lax.fori_loop(0, x_refs[0].shape[1] // TILE, x_step, 0, unroll=True)


def partial_logits(spots, own_rows, partner_rows, pair_gain, kept, received, cut, pieces):
    rows = own_rows.shape[0] * own_rows.shape[1] // 2
    wide, cols = kept.shape
    depth = 2 * wide
    whole = pl.BlockSpec(memory_space=pltpu.VMEM)
    x_shape = jax.ShapeDtypeStruct((rows // pieces, cols - cut), F32)
    return pl.pallas_call(
        logits_kernel,
        out_shape=[x_shape] * pieces + [jax.ShapeDtypeStruct((rows, cut + EXTRA), F32)],
        in_specs=[pl.BlockSpec(memory_space=pltpu.SMEM)] + [whole] * 5,
        out_specs=[whole] * (pieces + 1),
        scratch_shapes=[pltpu.VMEM((rows, depth), BF16), pltpu.VMEM((rows, depth), BF16)],
        compiler_params=pltpu.CompilerParams(vmem_limit_bytes=40 * 2**20),
        cost_estimate=pl.CostEstimate(
            flops=2 * rows * depth * cols, bytes_accessed=12 * 2**20, transcendentals=0
        ),
    )(spots, own_rows, partner_rows, pair_gain[None], kept, received)


def split_kernel(core_ref, head_ref, kept_ref, given_ref):
    cols = kept_ref.shape[1]
    mine = pl.multiple_of(core_ref[0] * cols, cols)
    other = pl.multiple_of((1 - core_ref[0]) * cols, cols)
    kept_ref[...] = head_ref[:, pl.ds(mine, cols)]
    given_ref[...] = head_ref[:, pl.ds(other, cols)]


def split_head(core, head_weight):
    depth, cols = head_weight.shape
    size = 128
    part = jax.ShapeDtypeStruct((depth, cols // 2), BF16)
    spec = pl.BlockSpec((size, cols // 2), lambda i: (i, 0))
    return pl.pallas_call(
        split_kernel,
        grid=(depth // size,),
        out_shape=(part, part),
        in_specs=[
            pl.BlockSpec(memory_space=pltpu.SMEM),
            pl.BlockSpec((size, cols), lambda i: (i, 0)),
        ],
        out_specs=(spec, spec),
        compiler_params=pltpu.CompilerParams(vmem_limit_bytes=16 * 2**20),
        cost_estimate=pl.CostEstimate(
            flops=10**10, bytes_accessed=4 * depth * cols, transcendentals=0
        ),
    )(core.astype(jnp.int32).reshape(1), head_weight)


def shards(hidden, norm_gain, head_weight, targets, exit_layer, loss_num, loss_den):
    yl, core, yh, z, x = (lax.axis_index(name) for name in AXES)
    vocab = yh * 8 + z
    group = (yl * 2 + core) * 4 + x
    own = hidden[0]
    tok, wide = own.shape
    cols = head_weight.shape[1] // 2
    width = 16 * wide
    gain = norm_gain.astype(F32)
    weight = exit_weights(exit_layer, loss_num, loss_den)

    pair_targets = jnp.stack(in_pair(targets[0], swap_core(targets[0]), "core", 1))
    moved = transpose_groups(own)
    kept, given = split_head(core, head_weight)
    received = swap_core(given)
    feature_rows = lax.all_to_all(
        jnp.broadcast_to(moved[None], (16, tok, wide)), ("yh", "z"), 0, 0, tiled=True
    )
    partner_group = (yl * 2 + 1 - core) * 4 + x
    pair_gain = jnp.concatenate(
        [
            lax.dynamic_slice_in_dim(gain, group * wide, wide),
            lax.dynamic_slice_in_dim(gain, partner_group * wide, wide),
        ]
    )
    feature_rows, pair_targets, pair_gain = lax.optimization_barrier(
        (feature_rows, pair_targets, pair_gain)
    )
    partner_rows = swap_core(feature_rows)
    part = 2 * tok
    cut = (cols * 3 // 8) // TILE * TILE

    def partials(pairs, dy, pieces):
        spots = jnp.stack(
            [
                ((yl ^ to_y) * 2 + side) * 4 + ((x + to_x) & 3)
                for to_y, to_x, side in x_spots(pairs) + y_spots(dy)
            ]
        ).astype(jnp.int32)
        return partial_logits(
            spots, feature_rows, partner_rows, pair_gain, kept, received, cut, pieces
        )

    to_right, to_left, over = partials(SENT, 1, 2)
    right0, left1, own0, own1, near = partials(HELD, 0, 4)

    from_left, from_right = lax.optimization_barrier(
        (shift_x(to_right, 1), shift_x(to_left, -1))
    )
    right0, left1 = lax.optimization_barrier(
        (right0 + from_left[:part], left1 + from_right[:part])
    )
    own0 = own0 + from_right[part:]
    own1 = own1 + from_left[part:]
    own0 = own0 + shift_x(right0, 1)
    own1 = own1 + shift_x(left1, -1)
    near = near + swap_y(over)
    own0, own1, near = lax.optimization_barrier((own0, own1, near))

    from_left, from_right, from_over = lax.optimization_barrier(
        (shift_x(near[:part], 1), shift_x(near[part : 2 * part], -1), swap_y(own1[:tok]))
    )
    right = near[2 * part : 2 * part + tok] + from_left[:tok]
    left = near[2 * part + tok : 3 * part] + from_right[:tok]
    upper = near[3 * part : 3 * part + tok] + from_right[tok:]
    lower = near[3 * part + tok :] + from_left[tok:]
    right, left = lax.optimization_barrier((right, left))
    y_sum = jnp.concatenate([upper + shift_x(right, 1), lower + shift_x(left, -1)], 0)
    x_sum = own0 + jnp.concatenate([from_over, swap_y(own1[tok:])], 0)

    columns = vocab * (2 * cols) + core * cols + lax.broadcasted_iota(jnp.int32, (1, cols), 1)
    slab_weight = lax.dynamic_slice_in_dim(weight, yl * 2, 2)
    part_weight = jnp.broadcast_to(slab_weight[:, None], (2, tok)).reshape(part)

    pair_inv = lax.rsqrt(y_sum[:, cut] / width + EPS).reshape(2, tok)
    raw = jnp.concatenate([y_sum[:, :cut], x_sum], 1)
    logits = raw * pair_inv.reshape(part)[:, None]
    hit = columns == pair_targets.reshape(part)[:, None]
    peak = jnp.max(logits, axis=1)
    lowered = logits - peak[:, None]
    power = jnp.exp(lowered)
    total = jnp.sum(power, axis=1)
    moment = jnp.sum(power * lowered, axis=1)
    chosen = jnp.sum(jnp.where(hit, logits, 0.0), axis=1)
    top, total, moment, chosen = combine_stats(jnp.stack([peak, total, moment, chosen]))
    log_total = top + jnp.log(total)
    probability = jnp.exp(logits - log_total[:, None])
    own_inv = pair_inv.reshape(part)
    row_scale = part_weight * own_inv
    grad_logits = (row_scale[:, None] * (probability - hit.astype(F32))).astype(BF16)
    loss = part_weight * (log_total - chosen)
    slope = part_weight * (moment / total + (top - chosen)) * (own_inv * own_inv / width)

    blocks = gather_group(grad_logits)

    def assembled(dy):
        grads = jnp.zeros((2, 4, tok, cols), BF16)
        for dx in (0, -1, 1, 2):
            grads = lax.dynamic_update_slice(
                grads, blocks[dy, dx].reshape(2, 1, tok, cols), (0, (x + dx) & 3, 0, 0)
            )
        return grads.reshape(8 * tok, cols)

    def chip_rows(grads, tie):
        def partial(source):
            return lax.dot_general(
                grads, source, (((1,), (1,)), ((), ())), preferred_element_type=F32
            )

        for_partner, _ = lax.optimization_barrier((partial(received).astype(BF16), tie))
        for_own = lax.optimization_barrier(partial(kept))
        return for_own + swap_core(for_partner).astype(F32)

    near_grads, over_grads = assembled(0), assembled(1)
    near_rows = chip_rows(near_grads, blocks[1, 2])
    over_rows = chip_rows(over_grads, blocks[1, 2])
    chip_sum = jnp.concatenate(in_pair(near_rows, over_rows, "yl", 1), 0).astype(BF16)
    chip_sum, feature_rows = lax.optimization_barrier((chip_sum, feature_rows))
    returned = lax.all_to_all(chip_sum.reshape(16, tok, wide), ("yh", "z"), 0, 0, tiled=True)
    pair_f32 = jnp.concatenate([feature_rows, partner_rows], 2).astype(F32)
    scaled = (pair_f32 * pair_gain).astype(BF16).reshape(2, 8 * tok, 2 * wide)

    def head_part(side, grads):
        rows = lax.dynamic_index_in_dim(scaled, side, 0, False)
        return lax.dot_general(
            rows, grads, (((0,), (0,)), ((), ())), preferred_element_type=F32
        )

    head_grad = (head_part(yl, near_grads) + head_part(1 - yl, over_grads)).astype(BF16)
    head_grad, loss, slope = lax.optimization_barrier((head_grad, loss, slope))
    late = gather_rows(jnp.stack([loss, slope])[None])
    mean_loss = jnp.sum(late[:, 0]) / (4 * tok)
    all_slope = late[:, 1].reshape(2, 4, 2, tok).transpose(0, 2, 1, 3).reshape(16, tok)
    head_own = head_grad[:wide]
    head_other = swap_core(head_grad[wide:])
    grad_head = jnp.concatenate(in_pair(head_own, head_other, "core", 1), 1)

    moved_slope = lax.dynamic_index_in_dim(all_slope, vocab, 0, False)[:, None]
    shrink = moved.astype(F32) * moved_slope
    returned, shrink = lax.optimization_barrier((returned, shrink))
    feature_grad = jnp.sum(returned.astype(F32), axis=0)
    grad_hidden = pair_gain[:wide] * feature_grad - shrink
    grad_hidden, grad_head = lax.optimization_barrier(
        (transpose_groups(grad_hidden.astype(BF16)), grad_head)
    )
    return grad_hidden[None], grad_head, mean_loss


def solution(mesh):
    fine = Mesh(mesh.devices.reshape(2, 2, 2, 8, 4), AXES)
    slab, entry = ("yl", "core"), ("yh", "z")
    in_specs = (
        P(slab, "x", entry),
        P(),
        P(slab + ("x",), entry),
        P(slab, "x"),
        P(),
        P(),
        P(),
    )
    out_specs = (P(slab, "x", entry), P(slab + ("x",), entry), P())
    return jax.shard_map(shards, mesh=fine, in_specs=in_specs, out_specs=out_specs, check_vma=False)
```

```python
import jax
import jax.numpy as jnp
from jax import lax
from jax.experimental import pallas as pl
from jax.experimental.pallas import tpu as pltpu
from jax.sharding import Mesh, PartitionSpec as P

LAYERS = 80
EPS = 1e-05
F32 = jnp.float32
BF16 = jnp.bfloat16
AXES = ("yl", "core", "yh", "z", "x")
SWAP = [(0, 1), (1, 0)]


def place(group, vocab):
    return ((group // 4) * 16 + vocab) * 4 + group % 4


TRANSPOSE = [(place(g, v), place(v, g)) for g in range(16) for v in range(16)]


def transpose_groups(block):
    return lax.ppermute(block, AXES, TRANSPOSE)


def shift_x(block, step):
    return lax.ppermute(block, "x", [(i, (i + step) % 4) for i in range(4)])


def swap_y(block):
    return lax.ppermute(block, "yl", SWAP)


def swap_core(block):
    return lax.ppermute(block, "core", SWAP)


def flip(block, axis, bit, size):
    return lax.ppermute(block, axis, [(i, i ^ bit) for i in range(size)])


def in_pair(mine, other, axis, bit):
    high = (lax.axis_index(axis) & bit) > 0
    return jnp.where(high, other, mine), jnp.where(high, mine, other)


def exit_weights(exit_layer, loss_num, loss_den):
    ratio_value = loss_num.astype(F32) / loss_den.astype(F32)
    scale_value = ratio_value * jnp.exp2(exit_layer.astype(F32) / LAYERS)
    return scale_value * (scale_value.shape[0] / jnp.sum(scale_value))


def gather_group(block):
    half = block.shape[0] // 2
    left = shift_x(block, 1)
    right = shift_x(block, -1)
    over = swap_y(block)
    far = jnp.concatenate([shift_x(left[:half], 1), shift_x(right[half:], -1)])
    over_right = swap_y(right)
    over_left = shift_x(over, 1)
    over_far = jnp.concatenate([swap_y(far[:half]), shift_x(over_right[half:], -1)])
    return {
        (0, 0): block,
        (0, -1): left,
        (0, 1): right,
        (0, 2): far,
        (1, 0): over,
        (1, -1): over_left,
        (1, 1): over_right,
        (1, 2): over_far,
    }


def gather_rows(values):
    for axis, bit, size in (("x", 1, 4), ("x", 2, 4), ("yl", 1, 2)):
        values = jnp.concatenate(in_pair(values, flip(values, axis, bit, size), axis, bit), 0)
    return values


def combine_stats(stats):
    for axis, bit, size in (("core", 1, 2), ("z", 1, 8), ("z", 2, 8), ("z", 4, 8), ("yh", 1, 2)):
        low, high = in_pair(stats, flip(stats, axis, bit, size), axis, bit)
        top = jnp.maximum(low[0], high[0])
        low_gap, high_gap = low[0] - top, high[0] - top
        low_factor, high_factor = jnp.exp(low_gap), jnp.exp(high_gap)
        total = low[1] * low_factor + high[1] * high_factor
        moment = (low[2] + low[1] * low_gap) * low_factor
        moment = moment + (high[2] + high[1] * high_gap) * high_factor
        stats = jnp.stack([top, total, moment, low[3] + high[3]])
    return stats


EXTRA = 128
TILE = 256
SIDES = (0, 1)
SENT = ((0, 2), (1, 1), (1, 2), (0, -1))
HELD = ((0, 1), (1, -1), (0, 0), (1, 0))
Y_ORDER = ((2, 0), (1, 1), (2, 1), (-1, 0), (1, 0), (-1, 1), (0, 0), (0, 1))


def x_spots(pairs):
    return [(dy, dx, side) for dy, dx in pairs for side in SIDES]


def y_spots(dy):
    return [(dy, dx, side) for dx, side in Y_ORDER]


def logits_kernel(
    spot_ref, own_ref, partner_ref, gain_ref, kept_ref, received_ref, *refs
):
    *x_refs, y_ref, x_rows, y_rows = refs
    tok, wide = own_ref.shape[1:]
    cut = y_ref.shape[1] - EXTRA
    for index in range(8):
        x_spot, y_spot = spot_ref[index], spot_ref[8 + index]
        rows = pl.ds(index * tok, tok)
        squares = jnp.zeros((tok, 1), F32)
        for source, half in ((own_ref, 0), (partner_ref, 1)):
            lanes = pl.ds(half * wide, wide)
            gain = gain_ref[:, lanes]
            x_rows[rows, lanes] = (source[x_spot].astype(F32) * gain).astype(BF16)
            block = source[y_spot].astype(F32)
            y_rows[rows, lanes] = (block * gain).astype(BF16)
            squares = squares + jnp.sum(block * block, axis=1, keepdims=True)
        y_ref[rows, cut:] = jnp.broadcast_to(squares, (tok, EXTRA))

    def product(lhs_ref, rows, columns):
        first = jnp.dot(lhs_ref[rows, :wide], kept_ref[:, columns], preferred_element_type=F32)
        return first + jnp.dot(
            lhs_ref[rows, wide:], received_ref[:, columns], preferred_element_type=F32
        )

    def y_step(index, carry):
        lanes = pl.ds(pl.multiple_of(index * TILE, TILE), TILE)
        y_ref[:, lanes] = product(y_rows, slice(None), lanes)
        return carry

    def x_step(index, carry):
        lanes = pl.ds(pl.multiple_of(index * TILE, TILE), TILE)
        columns = pl.ds(pl.multiple_of(cut + index * TILE, TILE), TILE)
        out = product(x_rows, slice(None), columns)
        size = x_refs[0].shape[0]
        for place, x_ref in enumerate(x_refs):
            x_ref[:, lanes] = out[place * size : (place + 1) * size]
        return carry

    lax.fori_loop(0, cut // TILE, y_step, 0, unroll=True)
    lax.fori_loop(0, x_refs[0].shape[1] // TILE, x_step, 0, unroll=True)


def partial_logits(spots, own_rows, partner_rows, pair_gain, kept, received, cut, pieces):
    rows = own_rows.shape[0] * own_rows.shape[1] // 2
    wide, cols = kept.shape
    depth = 2 * wide
    whole = pl.BlockSpec(memory_space=pltpu.VMEM)
    x_shape = jax.ShapeDtypeStruct((rows // pieces, cols - cut), F32)
    return pl.pallas_call(
        logits_kernel,
        out_shape=[x_shape] * pieces + [jax.ShapeDtypeStruct((rows, cut + EXTRA), F32)],
        in_specs=[pl.BlockSpec(memory_space=pltpu.SMEM)] + [whole] * 5,
        out_specs=[whole] * (pieces + 1),
        scratch_shapes=[pltpu.VMEM((rows, depth), BF16), pltpu.VMEM((rows, depth), BF16)],
        compiler_params=pltpu.CompilerParams(vmem_limit_bytes=40 * 2**20),
        cost_estimate=pl.CostEstimate(
            flops=2 * rows * depth * cols, bytes_accessed=12 * 2**20, transcendentals=0
        ),
    )(spots, own_rows, partner_rows, pair_gain[None], kept, received)


def split_kernel(core_ref, head_ref, kept_ref, given_ref):
    cols = kept_ref.shape[1]
    mine = pl.multiple_of(core_ref[0] * cols, cols)
    other = pl.multiple_of((1 - core_ref[0]) * cols, cols)
    kept_ref[...] = head_ref[:, pl.ds(mine, cols)]
    given_ref[...] = head_ref[:, pl.ds(other, cols)]


def split_head(core, head_weight):
    depth, cols = head_weight.shape
    size = 128
    part = jax.ShapeDtypeStruct((depth, cols // 2), BF16)
    spec = pl.BlockSpec((size, cols // 2), lambda i: (i, 0))
    return pl.pallas_call(
        split_kernel,
        grid=(depth // size,),
        out_shape=(part, part),
        in_specs=[
            pl.BlockSpec(memory_space=pltpu.SMEM),
            pl.BlockSpec((size, cols), lambda i: (i, 0)),
        ],
        out_specs=(spec, spec),
        compiler_params=pltpu.CompilerParams(vmem_limit_bytes=16 * 2**20),
        cost_estimate=pl.CostEstimate(
            flops=10**10, bytes_accessed=4 * depth * cols, transcendentals=0
        ),
    )(core.astype(jnp.int32).reshape(1), head_weight)


def shards(hidden, norm_gain, head_weight, targets, exit_layer, loss_num, loss_den):
    yl, core, yh, z, x = (lax.axis_index(name) for name in AXES)
    vocab = yh * 8 + z
    group = (yl * 2 + core) * 4 + x
    own = hidden[0]
    tok, wide = own.shape
    cols = head_weight.shape[1] // 2
    width = 16 * wide
    gain = norm_gain.astype(F32)
    weight = exit_weights(exit_layer, loss_num, loss_den)

    pair_targets = jnp.stack(in_pair(targets[0], swap_core(targets[0]), "core", 1))
    moved = transpose_groups(own)
    kept, given = split_head(core, head_weight)
    received = swap_core(given)
    feature_rows = lax.all_to_all(
        jnp.broadcast_to(moved[None], (16, tok, wide)), ("yh", "z"), 0, 0, tiled=True
    )
    partner_group = (yl * 2 + 1 - core) * 4 + x
    pair_gain = jnp.concatenate(
        [
            lax.dynamic_slice_in_dim(gain, group * wide, wide),
            lax.dynamic_slice_in_dim(gain, partner_group * wide, wide),
        ]
    )
    feature_rows, pair_targets, pair_gain = lax.optimization_barrier(
        (feature_rows, pair_targets, pair_gain)
    )
    partner_rows = swap_core(feature_rows)
    part = 2 * tok
    cut = (cols * 3 // 8) // TILE * TILE

    def partials(pairs, dy, pieces):
        spots = jnp.stack(
            [
                ((yl ^ to_y) * 2 + side) * 4 + ((x + to_x) & 3)
                for to_y, to_x, side in x_spots(pairs) + y_spots(dy)
            ]
        ).astype(jnp.int32)
        return partial_logits(
            spots, feature_rows, partner_rows, pair_gain, kept, received, cut, pieces
        )

    to_right, to_left, over = partials(SENT, 1, 2)
    right0, left1, own0, own1, near = partials(HELD, 0, 4)

    from_left, from_right = lax.optimization_barrier(
        (shift_x(to_right, 1), shift_x(to_left, -1))
    )
    right0, left1 = lax.optimization_barrier(
        (right0 + from_left[:part], left1 + from_right[:part])
    )
    early0, early1 = from_right[part:], from_left[part:]
    late0, late1, near = lax.optimization_barrier(
        (shift_x(right0, 1), shift_x(left1, -1), near + swap_y(over))
    )
    own0 = own0 + early0 + late0
    own1 = own1 + early1 + late1

    from_left, from_right, from_over = lax.optimization_barrier(
        (shift_x(near[:part], 1), shift_x(near[part : 2 * part], -1), swap_y(own1[:tok]))
    )
    right = near[2 * part : 2 * part + tok] + from_left[:tok]
    left = near[2 * part + tok : 3 * part] + from_right[:tok]
    upper = near[3 * part : 3 * part + tok] + from_right[tok:]
    lower = near[3 * part + tok :] + from_left[tok:]
    right, left = lax.optimization_barrier((right, left))
    y_sum = jnp.concatenate([upper + shift_x(right, 1), lower + shift_x(left, -1)], 0)
    x_sum = own0 + jnp.concatenate([from_over, swap_y(own1[tok:])], 0)

    columns = vocab * (2 * cols) + core * cols + lax.broadcasted_iota(jnp.int32, (1, cols), 1)
    slab_weight = lax.dynamic_slice_in_dim(weight, yl * 2, 2)
    part_weight = jnp.broadcast_to(slab_weight[:, None], (2, tok)).reshape(part)

    pair_inv = lax.rsqrt(y_sum[:, cut] / width + EPS).reshape(2, tok)
    raw = jnp.concatenate([y_sum[:, :cut], x_sum], 1)
    logits = raw * pair_inv.reshape(part)[:, None]
    hit = columns == pair_targets.reshape(part)[:, None]
    peak = jnp.max(logits, axis=1)
    lowered = logits - peak[:, None]
    power = jnp.exp(lowered)
    total = jnp.sum(power, axis=1)
    moment = jnp.sum(power * lowered, axis=1)
    chosen = jnp.sum(jnp.where(hit, logits, 0.0), axis=1)
    top, total, moment, chosen = combine_stats(jnp.stack([peak, total, moment, chosen]))
    log_total = top + jnp.log(total)
    probability = jnp.exp(logits - log_total[:, None])
    own_inv = pair_inv.reshape(part)
    row_scale = part_weight * own_inv
    grad_logits = (row_scale[:, None] * (probability - hit.astype(F32))).astype(BF16)
    loss = part_weight * (log_total - chosen)
    slope = part_weight * (moment / total + (top - chosen)) * (own_inv * own_inv / width)

    blocks = gather_group(grad_logits)

    def assembled(dy):
        grads = jnp.zeros((2, 4, tok, cols), BF16)
        for dx in (0, -1, 1, 2):
            grads = lax.dynamic_update_slice(
                grads, blocks[dy, dx].reshape(2, 1, tok, cols), (0, (x + dx) & 3, 0, 0)
            )
        return grads.reshape(8 * tok, cols)

    def chip_rows(grads, tie):
        def partial(source):
            return lax.dot_general(
                grads, source, (((1,), (1,)), ((), ())), preferred_element_type=F32
            )

        for_partner, _ = lax.optimization_barrier((partial(received).astype(BF16), tie))
        for_own = lax.optimization_barrier(partial(kept))
        return for_own + swap_core(for_partner).astype(F32)

    near_grads, over_grads = assembled(0), assembled(1)
    near_rows = chip_rows(near_grads, blocks[1, 2])
    over_rows = chip_rows(over_grads, blocks[1, 2])
    chip_sum = jnp.concatenate(in_pair(near_rows, over_rows, "yl", 1), 0).astype(BF16)
    chip_sum, feature_rows = lax.optimization_barrier((chip_sum, feature_rows))
    returned = lax.all_to_all(chip_sum.reshape(16, tok, wide), ("yh", "z"), 0, 0, tiled=True)
    pair_f32 = jnp.concatenate([feature_rows, partner_rows], 2).astype(F32)
    scaled = (pair_f32 * pair_gain).astype(BF16).reshape(2, 8 * tok, 2 * wide)

    def head_part(side, grads):
        rows = lax.dynamic_index_in_dim(scaled, side, 0, False)
        return lax.dot_general(
            rows, grads, (((0,), (0,)), ((), ())), preferred_element_type=F32
        )

    head_grad = (head_part(yl, near_grads) + head_part(1 - yl, over_grads)).astype(BF16)
    head_grad, loss, slope = lax.optimization_barrier((head_grad, loss, slope))
    late = gather_rows(jnp.stack([loss, slope])[None])
    mean_loss = jnp.sum(late[:, 0]) / (4 * tok)
    all_slope = late[:, 1].reshape(2, 4, 2, tok).transpose(0, 2, 1, 3).reshape(16, tok)
    head_own = head_grad[:wide]
    head_other = swap_core(head_grad[wide:])
    grad_head = jnp.concatenate(in_pair(head_own, head_other, "core", 1), 1)

    moved_slope = lax.dynamic_index_in_dim(all_slope, vocab, 0, False)[:, None]
    shrink = moved.astype(F32) * moved_slope
    returned, shrink = lax.optimization_barrier((returned, shrink))
    feature_grad = jnp.sum(returned.astype(F32), axis=0)
    grad_hidden = pair_gain[:wide] * feature_grad - shrink
    grad_hidden, grad_head = lax.optimization_barrier(
        (transpose_groups(grad_hidden.astype(BF16)), grad_head)
    )
    return grad_hidden[None], grad_head, mean_loss


def solution(mesh):
    fine = Mesh(mesh.devices.reshape(2, 2, 2, 8, 4), AXES)
    slab, entry = ("yl", "core"), ("yh", "z")
    in_specs = (
        P(slab, "x", entry),
        P(),
        P(slab + ("x",), entry),
        P(slab, "x"),
        P(),
        P(),
        P(),
    )
    out_specs = (P(slab, "x", entry), P(slab + ("x",), entry), P())
    return jax.shard_map(shards, mesh=fine, in_specs=in_specs, out_specs=out_specs, check_vma=False)
```
